32 devices in a mesh: dp: 2 (over x), blk: 8 (over z, core), uly: 2 (over y).
Axes of the slice: x: 2, y: 2, z: 4, core: 2. Of those that a mesh axis runs over, the one named last changes fastest.
Arguments:
- queries: bfloat16 [4096, 4096], P(('dp', 'blk', 'uly')), parts along dimension 0, may hold values from -24 to 24
- keys: bfloat16 [4096, 1024], P(('dp', 'blk', 'uly')), parts along dimension 0, may hold values from -12 to 12
- values: bfloat16 [4096, 1024], P(('dp', 'blk', 'uly')), parts along dimension 0, may hold values from -6 to 6
- doc_lengths: int32 [10], P('dp'), parts along dimension 0, may hold values from 1 to 512, 2048 in all
Outputs:
- attended: bfloat16 [4096, 4096], P(('dp', 'blk', 'uly')), parts along dimension 0
The draws below stay inside these ranges and needn't reach their ends.
There are 2 independent parts, one for each index of `dp`. The reference program is written for one: setup_inputs(seed, part) draws one part's arguments, and reference() takes and returns one part's arrays. A program takes and returns all parts, laid end to end along the dimension named above; each array names one. Nothing has to cross between parts.
Inputs may be any that keep to these rules, and one draw needn't show every extreme that they name: `doc_lengths`: the 5 lengths sum to 2048; the longest is exactly 512.
All inputs are finite; a program needn't handle non-finite values.
Results may differ from the reference program's by a relative error of at most 0.0055.
Values may be sent and summed in bfloat16 or wider, within the bound.
A program may use at most 64 MiB of HBM per device.

```python
import math
import jax
import jax.numpy as jnp
import numpy as np
from jax import lax

QUERY_HEADS = 32
KEY_VALUE_HEADS = 8
HEAD_SIZE = 128
TOK_DEV = 128
CYCLE = 2
PACKED_TOKENS = 2048
DOC_MAX = 512
DOCS = 5
N_BLK = 8
N_ULY = 2


def broadcast_keys(key):
    starting_offset = jax.random.normal(jax.random.fold_in(key, 7), (PACKED_TOKENS, KEY_VALUE_HEADS * HEAD_SIZE), jnp.float32)
    result = starting_offset
    return jnp.clip(result, -12.0, 12.0)


def draw_keys(key, part):
    return broadcast_keys(key).astype(jnp.bfloat16)


def draw_queries(key, part):
    own = jax.random.normal(jax.random.fold_in(key, 11), (PACKED_TOKENS, QUERY_HEADS * HEAD_SIZE), jnp.float32)
    return jnp.clip(own, -24.0, 24.0).astype(jnp.bfloat16)


def levels(own_key, dims, cuts, low, largest):
    def one(position, shards_of):
        draws = jax.random.uniform(jax.random.fold_in(jax.random.fold_in(own_key, 6), position), (shards_of,), jnp.float32, low / len(cuts), largest / len(cuts))
        return jnp.repeat(jnp.exp(draws), dims[position] // shards_of).reshape((-1,) + (1,) * (len(dims) - position - 1))

    level = one(*cuts[0])
    for cut in cuts[1:]:
        level = level * one(*cut)
    return level


def split_up(count, total, limit, lean):
    weights = [(1 << 20) // math.isqrt(standing ** lean) + 1 for standing in range(2, count + 1)]
    spare, holding = total - limit - (count - 1), [1] * (count - 1)
    while spare > 0:
        free = [i for i in range(count - 1) if holding[i] < limit]
        whole, left = sum([weights[i] for i in free]), spare
        for i in free:
            addition = min(limit - holding[i], max(1, left * weights[i] // whole), spare)
            holding[i] = holding[i] + addition
            spare = spare - addition
    return np.array([limit] + holding)


def ragged_sizes(key, amount, total, limit, lean):
    if amount == 2:
        one = jax.random.randint(key, (), max(1, total - limit), min(limit, total - 1) + 1)
        return jnp.stack([one, total - one])
    sizes = jnp.asarray(split_up(amount, total, limit, lean), jnp.int32)
    twos = (amount - 1) // 2
    giver, taker = sizes[1:1 + 2 * twos:2], sizes[2:2 + 2 * twos:2]
    room = jnp.minimum(giver - 1, limit - taker)
    passed = jax.random.randint(jax.random.fold_in(key, 1), (twos,), 0, 1 << 20) % (room + 1)
    sizes = sizes.at[1:1 + 2 * twos:2].set(giver - passed).at[2:2 + 2 * twos:2].set(taker + passed)
    return sizes[jax.random.permutation(jax.random.fold_in(key, 2), amount)]


def centred(own_key, dims, width, reach, cuts=(), kind=jnp.bfloat16):
    array = width * jax.random.normal(own_key, dims, jnp.float32)
    if cuts:
        array = array * levels(own_key, dims, cuts, -0.22, 0.18)
    return jnp.clip(array, -reach, reach).astype(kind)


def setup_inputs(seed: int = 0, part: int = 0) -> dict:
    seeds = jax.random.split(jax.random.key(seed), 5)
    part_splits = jax.random.split(jax.random.fold_in(seeds[4], part), 5)
    queries = draw_queries(jax.random.fold_in(jax.random.fold_in(seeds[4], part), 71), part)
    keys = draw_keys(jax.random.fold_in(jax.random.fold_in(seeds[4], part), 71), part)
    values = centred(part_splits[2], (PACKED_TOKENS, KEY_VALUE_HEADS * HEAD_SIZE), 1.0, 6.0, ((0, 16),))
    doc_lengths = ragged_sizes(part_splits[3], DOCS, PACKED_TOKENS, DOC_MAX, 2).astype(jnp.int32)
    return {"queries": queries, "keys": keys, "values": values, "doc_lengths": doc_lengths}


NEG_FILL = -1e+30

def reference(queries, keys, values, doc_lengths):
    block = TOK_DEV * N_ULY
    token_extent = CYCLE * block
    query_group = QUERY_HEADS // KEY_VALUE_HEADS
    total_rows = queries.shape[0]
    ends = jnp.cumsum(doc_lengths)

    def doc_of(positions):
        return lax.optimization_barrier(jnp.sum((positions[:, None] >= ends[None, :]).astype(jnp.int32), axis=1))
    q_all = queries.reshape(total_rows, QUERY_HEADS, HEAD_SIZE)
    padded_keys = jnp.concatenate([jnp.zeros((token_extent, KEY_VALUE_HEADS * HEAD_SIZE), keys.dtype), keys], axis=0).reshape(-1, KEY_VALUE_HEADS, HEAD_SIZE)
    padded_values = jnp.concatenate([jnp.zeros((token_extent, KEY_VALUE_HEADS * HEAD_SIZE), values.dtype), values], axis=0).reshape(-1, KEY_VALUE_HEADS, HEAD_SIZE)
    scale = 1.0 / math.sqrt(HEAD_SIZE)
    rows = jnp.arange(block, dtype=jnp.int32)
    cols = jnp.arange(token_extent + block, dtype=jnp.int32)

    def one_block(index):
        start = (index * block).astype(jnp.int32)
        q_block = lax.dynamic_slice_in_dim(q_all, start, block, 0).astype(jnp.float32)
        k_block = jnp.repeat(lax.dynamic_slice_in_dim(padded_keys, start, token_extent + block, 0).astype(jnp.float32), query_group, axis=1)
        v_block = jnp.repeat(lax.dynamic_slice_in_dim(padded_values, start, token_extent + block, 0).astype(jnp.float32), query_group, axis=1)
        q_pos = start + rows
        k_pos = start - token_extent + cols
        allowed = (k_pos[None, :] <= q_pos[:, None]) & (k_pos[None, :] >= 0) & (doc_of(k_pos)[None, :] == doc_of(q_pos)[:, None])
        scores = jnp.einsum('qhd,khd->hqk', q_block, k_block, precision=lax.Precision.HIGHEST) * scale
        scores = jnp.where(allowed[None], scores, NEG_FILL)
        peak = lax.optimization_barrier(jnp.max(scores, axis=-1, keepdims=True))
        weights = jnp.where(allowed[None], jnp.exp(scores - peak), 0.0)
        total = lax.optimization_barrier(jnp.sum(weights, axis=-1))
        rounded = lax.optimization_barrier(weights.astype(jnp.bfloat16)).astype(jnp.float32)
        summed = jnp.einsum('hqk,khd->qhd', rounded, v_block, precision=lax.Precision.HIGHEST)
        result = summed / jnp.transpose(total)[:, :, None]
        return result.astype(jnp.bfloat16).reshape(block, QUERY_HEADS * HEAD_SIZE)
    blocks = lax.map(one_block, jnp.arange(N_BLK, dtype=jnp.int32))
    return blocks.reshape(total_rows, QUERY_HEADS * HEAD_SIZE)
```

```python
import functools
import math

import jax
import jax.numpy as jnp
from jax import lax
from jax.experimental import pallas as pl
from jax.experimental.pallas import tpu as pltpu
from jax.sharding import PartitionSpec as P

QUERY_HEADS = 32
KEY_VALUE_HEADS = 8
HEAD_SIZE = 128
CYCLE = 2
GROUP = QUERY_HEADS // KEY_VALUE_HEADS

NEG_FILL = -1e30
AHEAD = 3
ORDER_FOUR = (4, 1, 2, 3)

FOUR = (
    ((0, 4, None), (0, 1, None), (0, 2, None)),
    ((0, 4, None), (0, 1, None), (0, 2, None), (1, 2, None), (4, -1, 1)),
    ((0, 4, None), (0, 1, None), (1, 2, 0), (4, -2, None), (4, -1, 1), (3, -2, None)),
    ((0, 4, None), (1, 2, 0), (4, -1, None), (4, -2, None)),
)


def routes_for(uly, blocks):
    if CYCLE * uly == 4 and blocks % 4 == 0:
        return FOUR, ORDER_FOUR
    reach = CYCLE * uly
    direct = tuple((0, k, None) for k in range(1, reach + 1))
    return (direct,), tuple(range(1, reach + 1))


def kernel(
    uly, blocks, q_hbm, k_hbm, v_hbm, len_ref, out_hbm,
    q_ref, kv_ref, o_ref, bias_ref, load_sem, q_sem, out_sem, send_sem, recv_sem,
):
    rows = q_ref.shape[0]
    reach = CYCLE * uly
    routes, order = routes_for(uly, blocks)
    period = len(routes)
    b = lax.axis_index("blk") * uly + lax.axis_index("uly")
    role = lax.rem(b, period)

    def target(other):
        return {"blk": other // uly, "uly": lax.rem(other, uly)}

    def place(g, slot):
        return kv_ref.at[g, :, pl.ds((reach - slot) * rows, rows), :]

    def loads(g):
        cols = pl.ds(pl.multiple_of(g * HEAD_SIZE, HEAD_SIZE), HEAD_SIZE)
        here = pl.ds(reach * rows, rows)
        return [
            pltpu.make_async_copy(src.at[:, cols], kv_ref.at[g, i, here, :], load_sem.at[i, g])
            for i, src in enumerate((k_hbm, v_hbm))
        ]

    q_copy = pltpu.make_async_copy(q_hbm, q_ref, q_sem)

    @pl.loop(0, KEY_VALUE_HEADS)
    def _(g):
        for copy in loads(g):
            copy.start()

    q_copy.start()

    spans = sorted({abs(delta) for role_routes in routes for _, delta, _ in role_routes})
    barrier = pltpu.get_barrier_semaphore()
    expected = 0
    for span in spans:
        for other in (b + span, b - span):
            valid = (other >= 0) & (other < blocks)
            expected = expected + valid.astype(jnp.int32)

            @pl.when(valid)
            def _():
                pl.semaphore_signal(
                    barrier, inc=1, device_id=target(other), device_id_type=pl.DeviceIdType.MESH
                )

    for slot in range(1, reach + 1):

        @pl.when(b < slot)
        def _():
            @pl.loop(0, KEY_VALUE_HEADS)
            def _(g):
                kv_ref[g, :, pl.ds((reach - slot) * rows, rows), :] = jnp.zeros(
                    (2, rows, HEAD_SIZE), kv_ref.dtype
                )

    q_pos = b * rows + lax.broadcasted_iota(jnp.int32, (rows, 1), 0)
    first = jnp.zeros((rows, 1), jnp.int32)
    end = jnp.int32(0)
    for d in range(len_ref.shape[0]):
        end = end + len_ref[d]
        first = jnp.where(q_pos >= end, end, first)
    k_pos = (b - reach) * rows + lax.broadcasted_iota(jnp.int32, bias_ref.shape, 1)
    bias_ref[...] = jnp.where((k_pos <= q_pos) & (k_pos >= first), 0.0, NEG_FILL)

    pl.semaphore_wait(barrier, expected)

    def each_route(g, only, act):
        for r, role_routes in enumerate(routes):
            for n, (slot, delta, parity) in enumerate(role_routes):
                if slot not in only:
                    continue
                other = b + delta
                go = (role == r) & (b >= slot) & (other >= 0) & (other < blocks)
                if parity is not None:
                    go = go & (lax.rem(g, 2) == parity)

                @pl.when(go)
                def _():
                    act(
                        pltpu.make_async_remote_copy(
                            src_ref=place(g, slot),
                            dst_ref=place(g, slot + delta),
                            send_sem=send_sem.at[n, g],
                            recv_sem=recv_sem.at[slot + delta - 1, g],
                            device_id=target(other),
                            device_id_type=pl.DeviceIdType.MESH,
                        )
                    )

    def send_own(g):
        for copy in loads(g):
            copy.wait()
        each_route(g, (0,), lambda copy: copy.start())

    @pl.loop(0, AHEAD)
    def _(g):
        send_own(g)

    q_copy.wait()
    factor = math.log2(math.e) / math.sqrt(HEAD_SIZE)

    def out_copy(g):
        width = GROUP * HEAD_SIZE
        cols = pl.ds(pl.multiple_of(g * width, width), width)
        return pltpu.make_async_copy(o_ref.at[:, cols], out_hbm.at[:, cols], out_sem.at[g])

    @pl.loop(0, KEY_VALUE_HEADS)
    def _(g):
        @pl.when(g + AHEAD < KEY_VALUE_HEADS)
        def _():
            send_own(g + AHEAD)

        for slot in order:

            @pl.when(b >= slot)
            def _():
                pltpu.make_async_copy(
                    place(g, slot), place(g, slot), recv_sem.at[slot - 1, g]
                ).wait()

            each_route(g, (slot,), lambda copy: copy.start())

        keys = kv_ref[g, 0]
        values = kv_ref[g, 1]

        def cols(r):
            return pl.ds(pl.multiple_of((g * GROUP + r) * HEAD_SIZE, HEAD_SIZE), HEAD_SIZE)

        queries = jnp.concatenate([q_ref[:, cols(r)] for r in range(GROUP)], axis=0)
        scores = lax.dot_general(
            queries, keys, (((1,), (1,)), ((), ())), preferred_element_type=jnp.float32
        )
        parts, totals = [], []
        for r in range(GROUP):
            part = scores[r * rows:(r + 1) * rows] + bias_ref[...]
            peak = jnp.max(part, axis=1, keepdims=True)
            weights = jnp.exp2((part - peak) * factor)
            totals.append(jnp.sum(weights, axis=1, keepdims=True))
            parts.append(weights.astype(jnp.bfloat16))
        summed = jnp.dot(
            jnp.concatenate(parts, axis=0), values, preferred_element_type=jnp.float32
        )
        for r in range(GROUP):
            o_ref[:, cols(r)] = (summed[r * rows:(r + 1) * rows] / totals[r]).astype(o_ref.dtype)
        out_copy(g).start()

    @pl.loop(0, KEY_VALUE_HEADS)
    def _(g):
        each_route(g, tuple(range(reach + 1)), lambda copy: copy.wait_send())
        out_copy(g).wait()


def per_device(uly, blocks, queries, keys, values, doc_lengths):
    rows = queries.shape[0]
    reach = CYCLE * uly
    routes, _ = routes_for(uly, blocks)
    most = max(len(role_routes) for role_routes in routes)
    span = (reach + 1) * rows
    flops = 4 * rows * span * QUERY_HEADS * HEAD_SIZE
    any_space = pl.BlockSpec(memory_space=pl.ANY)
    return pl.pallas_call(
        functools.partial(kernel, uly, blocks),
        out_shape=jax.ShapeDtypeStruct(queries.shape, queries.dtype),
        in_specs=[any_space, any_space, any_space, pl.BlockSpec(memory_space=pltpu.SMEM)],
        out_specs=any_space,
        scratch_shapes=[
            pltpu.VMEM(queries.shape, queries.dtype),
            pltpu.VMEM((KEY_VALUE_HEADS, 2, span, HEAD_SIZE), keys.dtype),
            pltpu.VMEM(queries.shape, queries.dtype),
            pltpu.VMEM((rows, span), jnp.float32),
            pltpu.SemaphoreType.DMA((2, KEY_VALUE_HEADS)),
            pltpu.SemaphoreType.DMA,
            pltpu.SemaphoreType.DMA((KEY_VALUE_HEADS,)),
            pltpu.SemaphoreType.DMA((most, KEY_VALUE_HEADS)),
            pltpu.SemaphoreType.DMA((reach, KEY_VALUE_HEADS)),
        ],
        cost_estimate=pl.CostEstimate(
            flops=flops,
            bytes_accessed=2 * (queries.size * 2 + keys.size * 2),
            transcendentals=rows * span * QUERY_HEADS,
        ),
        compiler_params=pltpu.CompilerParams(
            collective_id=0, has_side_effects=True, vmem_limit_bytes=48 * 1024 * 1024
        ),
    )(queries, keys, values, doc_lengths)


def solution(mesh):
    in_specs = (
        P(("dp", "blk", "uly"), None),
        P(("dp", "blk", "uly"), None),
        P(("dp", "blk", "uly"), None),
        P("dp"),
    )
    out_specs = P(("dp", "blk", "uly"), None)
    uly = mesh.shape["uly"]
    blocks = mesh.shape["blk"] * uly
    return jax.shard_map(
        functools.partial(per_device, uly, blocks),
        mesh=mesh, in_specs=in_specs, out_specs=out_specs, check_vma=False,
    )
```

```python
import functools
import math

import jax
import jax.numpy as jnp
from jax import lax
from jax.experimental import pallas as pl
from jax.experimental.pallas import tpu as pltpu
from jax.sharding import PartitionSpec as P

QUERY_HEADS = 32
KEY_VALUE_HEADS = 8
HEAD_SIZE = 128
CYCLE = 2
GROUP = QUERY_HEADS // KEY_VALUE_HEADS

NEG_FILL = -1e30
AHEAD = 3

FOUR = (
    ((0, 4, None), (0, 1, None), (0, 2, None)),
    ((0, 4, None), (0, 1, None), (0, 2, None), (1, 2, None), (4, -1, 1)),
    ((0, 4, None), (0, 1, None), (1, 2, 0), (4, -2, None), (4, -1, 1), (3, -2, None)),
    ((0, 4, None), (1, 2, 0), (4, -1, None), (4, -2, None)),
)
FOUR_HOPS = (
    ((4,), (2, 3), (1,)),
    ((4, 1), (2, 3), ()),
    ((4, 1, 2), (3,), ()),
    ((4, 1, 2), (3,), ()),
)


def routes_for(uly, blocks):
    if CYCLE * uly == 4 and blocks % 4 == 0:
        return FOUR, FOUR_HOPS
    reach = CYCLE * uly
    direct = tuple((0, k, None) for k in range(1, reach + 1))
    return (direct,), ((tuple(range(1, reach + 1)),),)


def kernel(
    uly, blocks, q_hbm, k_hbm, v_hbm, len_hbm, out_hbm,
    q_ref, kv_ref, o_ref, bias_ref, len_ref,
    load_sem, q_sem, len_sem, out_sem, send_sem, recv_sem,
):
    rows = q_ref.shape[0]
    reach = CYCLE * uly
    routes, hops = routes_for(uly, blocks)
    period = len(routes)
    b = lax.axis_index("blk") * uly + lax.axis_index("uly")
    role = lax.rem(b, period)

    def target(other):
        return {"blk": other // uly, "uly": lax.rem(other, uly)}

    def place(g, slot):
        return kv_ref.at[g, :, pl.ds((reach - slot) * rows, rows), :]

    def loads(g):
        cols = pl.ds(pl.multiple_of(g * HEAD_SIZE, HEAD_SIZE), HEAD_SIZE)
        here = pl.ds(reach * rows, rows)
        return [
            pltpu.make_async_copy(src.at[:, cols], kv_ref.at[g, i, here, :], load_sem.at[i, g])
            for i, src in enumerate((k_hbm, v_hbm))
        ]

    q_copy = pltpu.make_async_copy(q_hbm, q_ref, q_sem)
    len_copy = pltpu.make_async_copy(len_hbm, len_ref, len_sem)

    @pl.loop(0, KEY_VALUE_HEADS)
    def _(g):
        for copy in loads(g):
            copy.start()

    len_copy.start()
    q_copy.start()

    spans = sorted({abs(delta) for role_routes in routes for _, delta, _ in role_routes})
    barrier = pltpu.get_barrier_semaphore()
    expected = 0
    for span in spans:
        for other in (b + span, b - span):
            valid = (other >= 0) & (other < blocks)
            expected = expected + valid.astype(jnp.int32)

            @pl.when(valid)
            def _():
                pl.semaphore_signal(
                    barrier, inc=1, device_id=target(other), device_id_type=pl.DeviceIdType.MESH
                )

    for slot in range(1, reach + 1):

        @pl.when(b < slot)
        def _():
            @pl.loop(0, KEY_VALUE_HEADS)
            def _(g):
                kv_ref[g, :, pl.ds((reach - slot) * rows, rows), :] = jnp.zeros(
                    (2, rows, HEAD_SIZE), kv_ref.dtype
                )

    pl.semaphore_wait(barrier, expected)

    def each_route(g, only, act, roles=None):
        for r, role_routes in enumerate(routes):
            if roles is not None and r not in roles:
                continue
            for n, (slot, delta, parity) in enumerate(role_routes):
                if slot not in only:
                    continue
                other = b + delta
                go = (role == r) & (b >= slot) & (other >= 0) & (other < blocks)
                if parity is not None:
                    go = go & (lax.rem(g, 2) == parity)

                @pl.when(go)
                def _():
                    act(
                        pltpu.make_async_remote_copy(
                            src_ref=place(g, slot),
                            dst_ref=place(g, slot + delta),
                            send_sem=send_sem.at[n, g],
                            recv_sem=recv_sem.at[slot + delta - 1, g],
                            device_id=target(other),
                            device_id_type=pl.DeviceIdType.MESH,
                        )
                    )

    def send_own(g):
        for copy in loads(g):
            copy.wait()
        each_route(g, (0,), lambda copy: copy.start())

    @pl.loop(0, AHEAD)
    def _(g):
        send_own(g)

    len_copy.wait()
    q_pos = b * rows + lax.broadcasted_iota(jnp.int32, (rows, 1), 0)
    first = jnp.zeros((rows, 1), jnp.int32)
    end = jnp.int32(0)
    for d in range(len_ref.shape[0]):
        end = end + len_ref[d]
        first = jnp.where(q_pos >= end, end, first)
    k_pos = (b - reach) * rows + lax.broadcasted_iota(jnp.int32, bias_ref.shape, 1)
    bias_ref[...] = jnp.where((k_pos <= q_pos) & (k_pos >= first), 0.0, NEG_FILL)

    q_copy.wait()
    factor = math.log2(math.e) / math.sqrt(HEAD_SIZE)

    def out_copy(g):
        width = GROUP * HEAD_SIZE
        cols = pl.ds(pl.multiple_of(g * width, width), width)
        return pltpu.make_async_copy(o_ref.at[:, cols], out_hbm.at[:, cols], out_sem.at[g])

    def receive(g, role_slots):
        for r, slots in enumerate(role_slots):
            for slot in slots:

                @pl.when((role == r) & (b >= slot))
                def _():
                    pltpu.make_async_copy(
                        place(g, slot), place(g, slot), recv_sem.at[slot - 1, g]
                    ).wait()

                each_route(g, (slot,), lambda copy: copy.start(), (r,))

    def attend(g):
        keys = kv_ref[g, 0]
        values = kv_ref[g, 1]

        def cols(r):
            return pl.ds(pl.multiple_of((g * GROUP + r) * HEAD_SIZE, HEAD_SIZE), HEAD_SIZE)

        queries = jnp.concatenate([q_ref[:, cols(r)] for r in range(GROUP)], axis=0)
        scores = lax.dot_general(
            queries, keys, (((1,), (1,)), ((), ())), preferred_element_type=jnp.float32
        )
        parts, totals = [], []
        for r in range(GROUP):
            part = scores[r * rows:(r + 1) * rows] + bias_ref[...]
            peak = jnp.max(part, axis=1, keepdims=True)
            weights = jnp.exp2((part - peak) * factor)
            totals.append(jnp.sum(weights, axis=1, keepdims=True))
            parts.append(weights.astype(jnp.bfloat16))
        summed = jnp.dot(
            jnp.concatenate(parts, axis=0), values, preferred_element_type=jnp.float32
        )
        for r in range(GROUP):
            o_ref[:, cols(r)] = (summed[r * rows:(r + 1) * rows] / totals[r]).astype(o_ref.dtype)
        out_copy(g).start()

    depth = max(len(stages) for stages in hops)
    lag = sum(
        jnp.where(role == r, max(h for h, slots in enumerate(stages) if slots), 0)
        for r, stages in enumerate(hops)
    )

    @pl.loop(0, KEY_VALUE_HEADS + depth - 1)
    def _(t):
        @pl.when(t + AHEAD < KEY_VALUE_HEADS)
        def _():
            send_own(t + AHEAD)

        for hop in range(depth):

            @pl.when((t >= hop) & (t - hop < KEY_VALUE_HEADS))
            def _():
                receive(t - hop, [stages[hop] for stages in hops])

        @pl.when((t >= lag) & (t - lag < KEY_VALUE_HEADS))
        def _():
            attend(t - lag)

    @pl.loop(0, KEY_VALUE_HEADS)
    def _(g):
        each_route(g, tuple(range(reach + 1)), lambda copy: copy.wait_send())
        out_copy(g).wait()


def per_device(uly, blocks, queries, keys, values, doc_lengths):
    rows = queries.shape[0]
    reach = CYCLE * uly
    routes, _ = routes_for(uly, blocks)
    most = max(len(role_routes) for role_routes in routes)
    span = (reach + 1) * rows
    flops = 4 * rows * span * QUERY_HEADS * HEAD_SIZE
    any_space = pl.BlockSpec(memory_space=pl.ANY)
    return pl.pallas_call(
        functools.partial(kernel, uly, blocks),
        out_shape=jax.ShapeDtypeStruct(queries.shape, queries.dtype),
        in_specs=[any_space, any_space, any_space, any_space],
        out_specs=any_space,
        scratch_shapes=[
            pltpu.VMEM(queries.shape, queries.dtype),
            pltpu.VMEM((KEY_VALUE_HEADS, 2, span, HEAD_SIZE), keys.dtype),
            pltpu.VMEM(queries.shape, queries.dtype),
            pltpu.VMEM((rows, span), jnp.float32),
            pltpu.SMEM(doc_lengths.shape, doc_lengths.dtype),
            pltpu.SemaphoreType.DMA((2, KEY_VALUE_HEADS)),
            pltpu.SemaphoreType.DMA,
            pltpu.SemaphoreType.DMA,
            pltpu.SemaphoreType.DMA((KEY_VALUE_HEADS,)),
            pltpu.SemaphoreType.DMA((most, KEY_VALUE_HEADS)),
            pltpu.SemaphoreType.DMA((reach, KEY_VALUE_HEADS)),
        ],
        cost_estimate=pl.CostEstimate(
            flops=flops,
            bytes_accessed=2 * (queries.size * 2 + keys.size * 2),
            transcendentals=rows * span * QUERY_HEADS,
        ),
        compiler_params=pltpu.CompilerParams(
            collective_id=0, has_side_effects=True, vmem_limit_bytes=60 * 1024 * 1024
        ),
    )(queries, keys, values, doc_lengths)


def solution(mesh):
    in_specs = (
        P(("dp", "blk", "uly"), None),
        P(("dp", "blk", "uly"), None),
        P(("dp", "blk", "uly"), None),
        P("dp"),
    )
    out_specs = P(("dp", "blk", "uly"), None)
    uly = mesh.shape["uly"]
    blocks = mesh.shape["blk"] * uly
    return jax.shard_map(
        functools.partial(per_device, uly, blocks),
        mesh=mesh, in_specs=in_specs, out_specs=out_specs, check_vma=False,
    )
```

```python
import functools
import math

import jax
import jax.numpy as jnp
from jax import lax
from jax.experimental import pallas as pl
from jax.experimental.pallas import tpu as pltpu
from jax.sharding import PartitionSpec as P

QUERY_HEADS = 32
KEY_VALUE_HEADS = 8
HEAD_SIZE = 128
CYCLE = 2
GROUP = QUERY_HEADS // KEY_VALUE_HEADS

NEG_FILL = -1e30
FAR_AHEAD = 5
NEAR_AHEAD = 2

FOUR = (
    ((0, 4, None), (0, 1, None), (0, 2, None)),
    ((0, 4, None), (0, 1, None), (0, 2, None), (1, 2, None), (4, -1, 1)),
    ((0, 4, None), (0, 1, None), (1, 2, 0), (4, -2, None), (4, -1, 1), (3, -2, None)),
    ((0, 4, None), (1, 2, 0), (4, -1, None), (4, -2, None)),
)
FOUR_HOPS = (
    ((4,), (2, 3), (1,)),
    ((4, 1), (2, 3), ()),
    ((4, 1, 2), (3,), ()),
    ((4, 1, 2), (3,), ()),
)


def routes_for(uly, blocks):
    if CYCLE * uly == 4 and blocks % 4 == 0:
        return FOUR, FOUR_HOPS
    reach = CYCLE * uly
    direct = tuple((0, k, None) for k in range(1, reach + 1))
    return (direct,), ((tuple(range(1, reach + 1)),),)


def kernel(
    uly, blocks, q_hbm, k_hbm, v_hbm, len_hbm, o_ref,
    q_ref, kv_ref, bias_ref, len_ref,
    load_sem, q_sem, len_sem, send_sem, recv_sem,
):
    rows = q_ref.shape[0]
    reach = CYCLE * uly
    routes, hops = routes_for(uly, blocks)
    period = len(routes)
    b = lax.axis_index("blk") * uly + lax.axis_index("uly")
    role = lax.rem(b, period)

    def target(other):
        return {"blk": other // uly, "uly": lax.rem(other, uly)}

    def place(g, slot):
        return kv_ref.at[g, :, pl.ds((reach - slot) * rows, rows), :]

    def loads(g):
        cols = pl.ds(pl.multiple_of(g * HEAD_SIZE, HEAD_SIZE), HEAD_SIZE)
        here = pl.ds(reach * rows, rows)
        return [
            pltpu.make_async_copy(src.at[:, cols], kv_ref.at[g, i, here, :], load_sem.at[i, g])
            for i, src in enumerate((k_hbm, v_hbm))
        ]

    q_copy = pltpu.make_async_copy(q_hbm, q_ref, q_sem)
    len_copy = pltpu.make_async_copy(len_hbm, len_ref, len_sem)

    @pl.loop(0, KEY_VALUE_HEADS)
    def _(g):
        for copy in loads(g):
            copy.start()

    len_copy.start()
    q_copy.start()

    spans = sorted({abs(delta) for role_routes in routes for _, delta, _ in role_routes})
    barrier = pltpu.get_barrier_semaphore()
    expected = 0
    for span in spans:
        for other in (b + span, b - span):
            valid = (other >= 0) & (other < blocks)
            expected = expected + valid.astype(jnp.int32)

            @pl.when(valid)
            def _():
                pl.semaphore_signal(
                    barrier, inc=1, device_id=target(other), device_id_type=pl.DeviceIdType.MESH
                )

    for slot in range(1, reach + 1):

        @pl.when(b < slot)
        def _():
            @pl.loop(0, KEY_VALUE_HEADS)
            def _(g):
                kv_ref[g, :, pl.ds((reach - slot) * rows, rows), :] = jnp.zeros(
                    (2, rows, HEAD_SIZE), kv_ref.dtype
                )

    pl.semaphore_wait(barrier, expected)

    def each_route(g, only, act, roles=None, far=None):
        for r, role_routes in enumerate(routes):
            if roles is not None and r not in roles:
                continue
            for n, (slot, delta, parity) in enumerate(role_routes):
                if slot not in only or (far is not None and far != (delta == reach)):
                    continue
                other = b + delta
                go = (role == r) & (b >= slot) & (other >= 0) & (other < blocks)
                if parity is not None:
                    go = go & (lax.rem(g, 2) == parity)

                @pl.when(go)
                def _():
                    act(
                        pltpu.make_async_remote_copy(
                            src_ref=place(g, slot),
                            dst_ref=place(g, slot + delta),
                            send_sem=send_sem.at[n, g],
                            recv_sem=recv_sem.at[slot + delta - 1, g],
                            device_id=target(other),
                            device_id_type=pl.DeviceIdType.MESH,
                        )
                    )

    def send_far(g):
        for copy in loads(g):
            copy.wait()
        each_route(g, (0,), lambda copy: copy.start(), far=True)

    def send_near(g):
        each_route(g, (0,), lambda copy: copy.start(), far=False)

    @pl.loop(0, FAR_AHEAD)
    def _(g):
        send_far(g)

        @pl.when(g < NEAR_AHEAD)
        def _():
            send_near(g)

    len_copy.wait()
    q_pos = b * rows + lax.broadcasted_iota(jnp.int32, (rows, 1), 0)
    first = jnp.zeros((rows, 1), jnp.int32)
    end = jnp.int32(0)
    for d in range(len_ref.shape[0]):
        end = end + len_ref[d]
        first = jnp.where(q_pos >= end, end, first)
    k_pos = (b - reach) * rows + lax.broadcasted_iota(jnp.int32, bias_ref.shape, 1)
    bias_ref[...] = jnp.where((k_pos <= q_pos) & (k_pos >= first), 0.0, NEG_FILL)

    q_copy.wait()
    factor = math.log2(math.e) / math.sqrt(HEAD_SIZE)

    def receive(g, role_slots):
        for r, slots in enumerate(role_slots):
            for slot in slots:

                @pl.when((role == r) & (b >= slot))
                def _():
                    pltpu.make_async_copy(
                        place(g, slot), place(g, slot), recv_sem.at[slot - 1, g]
                    ).wait()

                each_route(g, (slot,), lambda copy: copy.start(), (r,))

    def attend(g):
        keys = kv_ref[g, 0]
        values = kv_ref[g, 1]

        def cols(r):
            return pl.ds(pl.multiple_of((g * GROUP + r) * HEAD_SIZE, HEAD_SIZE), HEAD_SIZE)

        queries = jnp.concatenate([q_ref[:, cols(r)] for r in range(GROUP)], axis=0)
        scores = lax.dot_general(
            queries, keys, (((1,), (1,)), ((), ())), preferred_element_type=jnp.float32
        )
        parts = []
        for r in range(GROUP):
            part = scores[r * rows:(r + 1) * rows] + bias_ref[...]
            peak = jnp.max(part, axis=1, keepdims=True)
            parts.append(jnp.exp2((part - peak) * factor).astype(jnp.bfloat16))
        summed = jnp.dot(
            jnp.concatenate(parts, axis=0),
            jnp.concatenate([values, jnp.ones_like(values)], axis=1),
            preferred_element_type=jnp.float32,
        )
        result = (summed[:, :HEAD_SIZE] / summed[:, HEAD_SIZE:]).astype(o_ref.dtype)
        for r in range(GROUP):
            o_ref[:, cols(r)] = result[r * rows:(r + 1) * rows]

    depth = max(len(stages) for stages in hops)
    lag = sum(
        jnp.where(role == r, max(h for h, slots in enumerate(stages) if slots), 0)
        for r, stages in enumerate(hops)
    )

    @pl.loop(0, KEY_VALUE_HEADS + depth - 1)
    def _(t):
        @pl.when(t + FAR_AHEAD < KEY_VALUE_HEADS)
        def _():
            send_far(t + FAR_AHEAD)

        @pl.when(t + NEAR_AHEAD < KEY_VALUE_HEADS)
        def _():
            send_near(t + NEAR_AHEAD)

        for hop in range(depth):

            @pl.when((t >= hop) & (t - hop < KEY_VALUE_HEADS))
            def _():
                receive(t - hop, [stages[hop] for stages in hops])

        @pl.when((t >= lag) & (t - lag < KEY_VALUE_HEADS))
        def _():
            attend(t - lag)

    @pl.loop(0, KEY_VALUE_HEADS)
    def _(g):
        each_route(g, tuple(range(reach + 1)), lambda copy: copy.wait_send())


def per_device(uly, blocks, queries, keys, values, doc_lengths):
    rows = queries.shape[0]
    reach = CYCLE * uly
    routes, _ = routes_for(uly, blocks)
    most = max(len(role_routes) for role_routes in routes)
    span = (reach + 1) * rows
    flops = 4 * rows * span * QUERY_HEADS * HEAD_SIZE
    return pl.pallas_call(
        functools.partial(kernel, uly, blocks),
        out_shape=pltpu.VMEM(queries.shape, queries.dtype),
        in_specs=[pl.BlockSpec(memory_space=pl.ANY)] * 4,
        out_specs=pl.BlockSpec(memory_space=pltpu.VMEM),
        scratch_shapes=[
            pltpu.VMEM(queries.shape, queries.dtype),
            pltpu.VMEM((KEY_VALUE_HEADS, 2, span, HEAD_SIZE), keys.dtype),
            pltpu.VMEM((rows, span), jnp.float32),
            pltpu.SMEM(doc_lengths.shape, doc_lengths.dtype),
            pltpu.SemaphoreType.DMA((2, KEY_VALUE_HEADS)),
            pltpu.SemaphoreType.DMA,
            pltpu.SemaphoreType.DMA,
            pltpu.SemaphoreType.DMA((most, KEY_VALUE_HEADS)),
            pltpu.SemaphoreType.DMA((reach, KEY_VALUE_HEADS)),
        ],
        cost_estimate=pl.CostEstimate(
            flops=flops,
            bytes_accessed=2 * (queries.size * 2 + keys.size * 2),
            transcendentals=rows * span * QUERY_HEADS,
        ),
        compiler_params=pltpu.CompilerParams(
            collective_id=0, has_side_effects=True, vmem_limit_bytes=60 * 1024 * 1024
        ),
    )(queries, keys, values, doc_lengths)


def solution(mesh):
    in_specs = (
        P(("dp", "blk", "uly"), None),
        P(("dp", "blk", "uly"), None),
        P(("dp", "blk", "uly"), None),
        P("dp"),
    )
    out_specs = P(("dp", "blk", "uly"), None)
    uly = mesh.shape["uly"]
    blocks = mesh.shape["blk"] * uly
    return jax.shard_map(
        functools.partial(per_device, uly, blocks),
        mesh=mesh, in_specs=in_specs, out_specs=out_specs, check_vma=False,
    )
```

```python
import functools
import math

import jax
import jax.numpy as jnp
from jax import lax
from jax.experimental import pallas as pl
from jax.experimental.pallas import tpu as pltpu
from jax.sharding import PartitionSpec as P

QUERY_HEADS = 32
KEY_VALUE_HEADS = 8
HEAD_SIZE = 128
CYCLE = 2
GROUP = QUERY_HEADS // KEY_VALUE_HEADS

NEG_FILL = -1e30
FAR_AHEAD = (1, 2, 3, 4)
NEAR_AHEAD = 2

FOUR = (
    ((0, 4, None), (0, 1, None), (0, 2, None)),
    ((0, 4, None), (0, 1, None), (0, 2, None), (1, 2, None), (4, -1, 1)),
    ((0, 4, None), (0, 1, None), (1, 2, 0), (4, -2, None), (4, -1, 1), (3, -2, None)),
    ((0, 4, None), (1, 2, 0), (4, -1, None), (4, -2, None)),
)
FOUR_HOPS = (
    ((), (), (4, 2, 3, 1)),
    ((4, 1), (2, 3), ()),
    ((4, 1), (2, 3), ()),
    ((4, 1), (2, 3), ()),
)


def routes_for(uly, blocks):
    if CYCLE * uly == 4 and blocks % 4 == 0:
        return FOUR, FOUR_HOPS
    reach = CYCLE * uly
    direct = tuple((0, k, None) for k in range(1, reach + 1))
    return (direct,), ((tuple(range(1, reach + 1)),),)


def kernel(
    uly, blocks, q_hbm, k_hbm, v_hbm, len_hbm, o_ref,
    q_ref, kv_ref, bias_ref, len_ref,
    load_sem, q_sem, len_sem, send_sem, recv_sem,
):
    rows = q_ref.shape[0]
    reach = CYCLE * uly
    routes, hops = routes_for(uly, blocks)
    period = len(routes)
    b = lax.axis_index("blk") * uly + lax.axis_index("uly")
    role = lax.rem(b, period)

    def target(other):
        return {"blk": other // uly, "uly": lax.rem(other, uly)}

    def place(g, slot):
        return kv_ref.at[g, :, pl.ds((reach - slot) * rows, rows), :]

    def loads(g):
        cols = pl.ds(pl.multiple_of(g * HEAD_SIZE, HEAD_SIZE), HEAD_SIZE)
        here = pl.ds(reach * rows, rows)
        return [
            pltpu.make_async_copy(src.at[:, cols], kv_ref.at[g, i, here, :], load_sem.at[i, g])
            for i, src in enumerate((k_hbm, v_hbm))
        ]

    q_copy = pltpu.make_async_copy(q_hbm, q_ref, q_sem)
    len_copy = pltpu.make_async_copy(len_hbm, len_ref, len_sem)

    @pl.loop(0, KEY_VALUE_HEADS)
    def _(g):
        for copy in loads(g):
            copy.start()

    len_copy.start()
    q_copy.start()

    spans = sorted({abs(delta) for role_routes in routes for _, delta, _ in role_routes})
    barrier = pltpu.get_barrier_semaphore()
    expected = 0
    for span in spans:
        for other in (b + span, b - span):
            valid = (other >= 0) & (other < blocks)
            expected = expected + valid.astype(jnp.int32)

            @pl.when(valid)
            def _():
                pl.semaphore_signal(
                    barrier, inc=1, device_id=target(other), device_id_type=pl.DeviceIdType.MESH
                )

    for slot in range(1, reach + 1):

        @pl.when(b < slot)
        def _():
            @pl.loop(0, KEY_VALUE_HEADS)
            def _(g):
                kv_ref[g, :, pl.ds((reach - slot) * rows, rows), :] = jnp.zeros(
                    (2, rows, HEAD_SIZE), kv_ref.dtype
                )

    pl.semaphore_wait(barrier, expected)

    def each_route(g, only, act, roles=None, far=None):
        for r, role_routes in enumerate(routes):
            if roles is not None and r not in roles:
                continue
            for n, (slot, delta, parity) in enumerate(role_routes):
                if slot not in only or (far is not None and far != (delta == reach)):
                    continue
                other = b + delta
                go = (role == r) & (b >= slot) & (other >= 0) & (other < blocks)
                if parity is not None:
                    go = go & (lax.rem(g, 2) == parity)

                @pl.when(go)
                def _():
                    act(
                        pltpu.make_async_remote_copy(
                            src_ref=place(g, slot),
                            dst_ref=place(g, slot + delta),
                            send_sem=send_sem.at[n, g],
                            recv_sem=recv_sem.at[slot + delta - 1, g],
                            device_id=target(other),
                            device_id_type=pl.DeviceIdType.MESH,
                        )
                    )

    @pl.loop(0, KEY_VALUE_HEADS)
    def _(g):
        for copy in loads(g):
            copy.wait()

    def send_far(g):
        each_route(g, (0,), lambda copy: copy.start(), far=True)

    def send_near(g):
        each_route(g, (0,), lambda copy: copy.start(), far=False)

    far_ahead = sum(jnp.where(role == r, FAR_AHEAD[r], 0) for r in range(period))

    @pl.loop(0, max(NEAR_AHEAD, *FAR_AHEAD))
    def _(g):
        @pl.when(g < far_ahead)
        def _():
            send_far(g)

        @pl.when(g < NEAR_AHEAD)
        def _():
            send_near(g)

    len_copy.wait()
    q_pos = b * rows + lax.broadcasted_iota(jnp.int32, (rows, 1), 0)
    first = jnp.zeros((rows, 1), jnp.int32)
    end = jnp.int32(0)
    for d in range(len_ref.shape[0]):
        end = end + len_ref[d]
        first = jnp.where(q_pos >= end, end, first)
    k_pos = (b - reach) * rows + lax.broadcasted_iota(jnp.int32, bias_ref.shape, 1)
    bias_ref[...] = jnp.where((k_pos <= q_pos) & (k_pos >= first), 0.0, NEG_FILL)

    q_copy.wait()
    factor = math.log2(math.e) / math.sqrt(HEAD_SIZE)

    def receive(g, role_slots):
        for r, slots in enumerate(role_slots):
            for slot in slots:

                @pl.when((role == r) & (b >= slot))
                def _():
                    pltpu.make_async_copy(
                        place(g, slot), place(g, slot), recv_sem.at[slot - 1, g]
                    ).wait()

                each_route(g, (slot,), lambda copy: copy.start(), (r,))

    def attend(g):
        keys = kv_ref[g, 0]
        values = kv_ref[g, 1]

        def cols(r):
            return pl.ds(pl.multiple_of((g * GROUP + r) * HEAD_SIZE, HEAD_SIZE), HEAD_SIZE)

        queries = jnp.concatenate([q_ref[:, cols(r)] for r in range(GROUP)], axis=0)
        scores = lax.dot_general(
            queries, keys, (((1,), (1,)), ((), ())), preferred_element_type=jnp.float32
        )
        parts = []
        for r in range(GROUP):
            part = scores[r * rows:(r + 1) * rows] + bias_ref[...]
            peak = jnp.max(part, axis=1, keepdims=True)
            parts.append(jnp.exp2((part - peak) * factor).astype(jnp.bfloat16))
        summed = jnp.dot(
            jnp.concatenate(parts, axis=0),
            jnp.concatenate([values, jnp.ones_like(values)], axis=1),
            preferred_element_type=jnp.float32,
        )
        result = (summed[:, :HEAD_SIZE] / summed[:, HEAD_SIZE:]).astype(o_ref.dtype)
        for r in range(GROUP):
            o_ref[:, cols(r)] = result[r * rows:(r + 1) * rows]

    depth = max(len(stages) for stages in hops)
    lag = sum(
        jnp.where(role == r, max(h for h, slots in enumerate(stages) if slots), 0)
        for r, stages in enumerate(hops)
    )

    @pl.loop(0, KEY_VALUE_HEADS + depth - 1)
    def _(t):
        @pl.when(t + far_ahead < KEY_VALUE_HEADS)
        def _():
            send_far(t + far_ahead)

        @pl.when(t + NEAR_AHEAD < KEY_VALUE_HEADS)
        def _():
            send_near(t + NEAR_AHEAD)

        for hop in range(depth):

            @pl.when((t >= hop) & (t - hop < KEY_VALUE_HEADS))
            def _():
                receive(t - hop, [stages[hop] for stages in hops])

        @pl.when((t >= lag) & (t - lag < KEY_VALUE_HEADS))
        def _():
            attend(t - lag)

    @pl.loop(0, KEY_VALUE_HEADS)
    def _(g):
        each_route(g, tuple(range(reach + 1)), lambda copy: copy.wait_send())


def per_device(uly, blocks, queries, keys, values, doc_lengths):
    rows = queries.shape[0]
    reach = CYCLE * uly
    routes, _ = routes_for(uly, blocks)
    most = max(len(role_routes) for role_routes in routes)
    span = (reach + 1) * rows
    flops = 4 * rows * span * QUERY_HEADS * HEAD_SIZE
    return pl.pallas_call(
        functools.partial(kernel, uly, blocks),
        out_shape=pltpu.VMEM(queries.shape, queries.dtype),
        in_specs=[pl.BlockSpec(memory_space=pl.ANY)] * 4,
        out_specs=pl.BlockSpec(memory_space=pltpu.VMEM),
        scratch_shapes=[
            pltpu.VMEM(queries.shape, queries.dtype),
            pltpu.VMEM((KEY_VALUE_HEADS, 2, span, HEAD_SIZE), keys.dtype),
            pltpu.VMEM((rows, span), jnp.float32),
            pltpu.SMEM(doc_lengths.shape, doc_lengths.dtype),
            pltpu.SemaphoreType.DMA((2, KEY_VALUE_HEADS)),
            pltpu.SemaphoreType.DMA,
            pltpu.SemaphoreType.DMA,
            pltpu.SemaphoreType.DMA((most, KEY_VALUE_HEADS)),
            pltpu.SemaphoreType.DMA((reach, KEY_VALUE_HEADS)),
        ],
        cost_estimate=pl.CostEstimate(
            flops=flops,
            bytes_accessed=2 * (queries.size * 2 + keys.size * 2),
            transcendentals=rows * span * QUERY_HEADS,
        ),
        compiler_params=pltpu.CompilerParams(
            collective_id=0, has_side_effects=True, vmem_limit_bytes=60 * 1024 * 1024
        ),
    )(queries, keys, values, doc_lengths)


def solution(mesh):
    in_specs = (
        P(("dp", "blk", "uly"), None),
        P(("dp", "blk", "uly"), None),
        P(("dp", "blk", "uly"), None),
        P("dp"),
    )
    out_specs = P(("dp", "blk", "uly"), None)
    uly = mesh.shape["uly"]
    blocks = mesh.shape["blk"] * uly
    return jax.shard_map(
        functools.partial(per_device, uly, blocks),
        mesh=mesh, in_specs=in_specs, out_specs=out_specs, check_vma=False,
    )
```

```python
import functools
import math

import jax
import jax.numpy as jnp
from jax import lax
from jax.experimental import pallas as pl
from jax.experimental.pallas import tpu as pltpu
from jax.sharding import PartitionSpec as P

QUERY_HEADS = 32
KEY_VALUE_HEADS = 8
HEAD_SIZE = 128
CYCLE = 2
GROUP = QUERY_HEADS // KEY_VALUE_HEADS

NEG_FILL = -1e30
AHEAD = 3

FOUR = (
    ((0, 4, None), (0, 1, None), (0, 2, None)),
    ((0, 4, None), (0, 1, None), (0, 2, None), (1, 2, None), (4, -1, 1)),
    ((0, 4, None), (0, 1, None), (1, 2, 0), (4, -2, None), (4, -1, 1), (3, -2, None)),
    ((0, 4, None), (1, 2, 0), (4, -1, None), (4, -2, None)),
)
FOUR_HOPS = (
    ((4,), (2, 3), (1,)),
    ((4, 1), (2, 3), ()),
    ((4, 1, 2), (3,), ()),
    ((4, 1, 2), (3,), ()),
)


def routes_for(uly, blocks):
    if CYCLE * uly == 4 and blocks % 4 == 0:
        return FOUR, FOUR_HOPS
    reach = CYCLE * uly
    direct = tuple((0, k, None) for k in range(1, reach + 1))
    return (direct,), ((tuple(range(1, reach + 1)),),)


def kernel(
    uly, blocks, q_hbm, k_hbm, v_hbm, len_hbm, o_ref,
    q_ref, kv_ref, bias_ref, len_ref,
    load_sem, q_sem, len_sem, send_sem, recv_sem,
):
    rows = q_ref.shape[0]
    reach = CYCLE * uly
    routes, hops = routes_for(uly, blocks)
    period = len(routes)
    b = lax.axis_index("blk") * uly + lax.axis_index("uly")
    role = lax.rem(b, period)

    def target(other):
        return {"blk": other // uly, "uly": lax.rem(other, uly)}

    def place(g, slot):
        return kv_ref.at[g, :, pl.ds((reach - slot) * rows, rows), :]

    def loads(g):
        cols = pl.ds(pl.multiple_of(g * HEAD_SIZE, HEAD_SIZE), HEAD_SIZE)
        here = pl.ds(reach * rows, rows)
        return [
            pltpu.make_async_copy(src.at[:, cols], kv_ref.at[g, i, here, :], load_sem.at[i, g])
            for i, src in enumerate((k_hbm, v_hbm))
        ]

    q_copy = pltpu.make_async_copy(q_hbm, q_ref, q_sem)
    len_copy = pltpu.make_async_copy(len_hbm, len_ref, len_sem)

    @pl.loop(0, KEY_VALUE_HEADS)
    def _(g):
        for copy in loads(g):
            copy.start()

    len_copy.start()
    q_copy.start()

    spans = sorted({abs(delta) for role_routes in routes for _, delta, _ in role_routes})
    barrier = pltpu.get_barrier_semaphore()
    expected = 0
    for span in spans:
        for other in (b + span, b - span):
            valid = (other >= 0) & (other < blocks)
            expected = expected + valid.astype(jnp.int32)

            @pl.when(valid)
            def _():
                pl.semaphore_signal(
                    barrier, inc=1, device_id=target(other), device_id_type=pl.DeviceIdType.MESH
                )

    for slot in range(1, reach + 1):

        @pl.when(b < slot)
        def _():
            @pl.loop(0, KEY_VALUE_HEADS)
            def _(g):
                kv_ref[g, :, pl.ds((reach - slot) * rows, rows), :] = jnp.zeros(
                    (2, rows, HEAD_SIZE), kv_ref.dtype
                )

    pl.semaphore_wait(barrier, expected)

    def start(r, g, from_slot):
        for n, (slot, delta, parity) in enumerate(routes[r]):
            if slot != from_slot:
                continue
            other = b + delta
            go = (other >= 0) & (other < blocks)
            if parity is not None:
                go = go & (lax.rem(g, 2) == parity)

            @pl.when(go)
            def _():
                pltpu.make_async_remote_copy(
                    src_ref=place(g, slot),
                    dst_ref=place(g, slot + delta),
                    send_sem=send_sem.at[n],
                    recv_sem=recv_sem.at[slot + delta - 1, g],
                    device_id=target(other),
                    device_id_type=pl.DeviceIdType.MESH,
                ).start()

    def receive(r, g, slots):
        for slot in slots:

            @pl.when(b >= slot)
            def _():
                pltpu.make_async_copy(
                    place(g, slot), place(g, slot), recv_sem.at[slot - 1, g]
                ).wait()
                start(r, g, slot)

    def all_sent(r):
        for n, (slot, delta, parity) in enumerate(routes[r]):
            other = b + delta
            heads = KEY_VALUE_HEADS if parity is None else KEY_VALUE_HEADS // 2

            @pl.when((b >= slot) & (other >= 0) & (other < blocks))
            def _():
                sent = kv_ref.at[pl.ds(0, heads), :, pl.ds((reach - slot) * rows, rows), :]
                pltpu.make_async_copy(sent, sent, send_sem.at[n]).wait()

    @pl.loop(0, KEY_VALUE_HEADS)
    def _(g):
        for copy in loads(g):
            copy.wait()

    for r in range(period):

        @pl.when(role == r)
        def _():
            @pl.loop(0, AHEAD)
            def _(g):
                start(r, g, 0)

    len_copy.wait()
    q_pos = b * rows + lax.broadcasted_iota(jnp.int32, (rows, 1), 0)
    first = jnp.zeros((rows, 1), jnp.int32)
    end = jnp.int32(0)
    for d in range(len_ref.shape[0]):
        end = end + len_ref[d]
        first = jnp.where(q_pos >= end, end, first)
    k_pos = (b - reach) * rows + lax.broadcasted_iota(jnp.int32, bias_ref.shape, 1)
    bias_ref[...] = jnp.where((k_pos <= q_pos) & (k_pos >= first), 0.0, NEG_FILL)

    q_copy.wait()
    factor = math.log2(math.e) / math.sqrt(HEAD_SIZE)

    def attend(g):
        keys = kv_ref[g, 0]
        values = kv_ref[g, 1]

        def cols(r):
            return pl.ds(pl.multiple_of((g * GROUP + r) * HEAD_SIZE, HEAD_SIZE), HEAD_SIZE)

        queries = jnp.concatenate([q_ref[:, cols(r)] for r in range(GROUP)], axis=0)
        scores = lax.dot_general(
            queries, keys, (((1,), (1,)), ((), ())), preferred_element_type=jnp.float32
        )
        parts = []
        for r in range(GROUP):
            part = scores[r * rows:(r + 1) * rows] + bias_ref[...]
            peak = jnp.max(part, axis=1, keepdims=True)
            parts.append(jnp.exp2((part - peak) * factor).astype(jnp.bfloat16))
        summed = jnp.dot(
            jnp.concatenate(parts, axis=0),
            jnp.concatenate([values, jnp.ones_like(values)], axis=1),
            preferred_element_type=jnp.float32,
        )
        result = (summed[:, :HEAD_SIZE] / summed[:, HEAD_SIZE:]).astype(o_ref.dtype)
        for r in range(GROUP):
            o_ref[:, cols(r)] = result[r * rows:(r + 1) * rows]

    depth = max(len(stages) for stages in hops)
    lag = sum(
        jnp.where(role == r, max(h for h, slots in enumerate(stages) if slots), 0)
        for r, stages in enumerate(hops)
    )

    @pl.loop(0, KEY_VALUE_HEADS + depth - 1)
    def _(t):
        for r, stages in enumerate(hops):

            @pl.when(role == r)
            def _():
                @pl.when(t + AHEAD < KEY_VALUE_HEADS)
                def _():
                    start(r, t + AHEAD, 0)

                for hop, slots in enumerate(stages):
                    if slots:

                        @pl.when((t >= hop) & (t - hop < KEY_VALUE_HEADS))
                        def _():
                            receive(r, t - hop, slots)

        @pl.when((t >= lag) & (t - lag < KEY_VALUE_HEADS))
        def _():
            attend(t - lag)

    for r in range(period):

        @pl.when(role == r)
        def _():
            all_sent(r)


def per_device(uly, blocks, queries, keys, values, doc_lengths):
    rows = queries.shape[0]
    reach = CYCLE * uly
    routes, _ = routes_for(uly, blocks)
    most = max(len(role_routes) for role_routes in routes)
    span = (reach + 1) * rows
    flops = 4 * rows * span * QUERY_HEADS * HEAD_SIZE
    return pl.pallas_call(
        functools.partial(kernel, uly, blocks),
        out_shape=pltpu.VMEM(queries.shape, queries.dtype),
        in_specs=[pl.BlockSpec(memory_space=pl.ANY)] * 4,
        out_specs=pl.BlockSpec(memory_space=pltpu.VMEM),
        scratch_shapes=[
            pltpu.VMEM(queries.shape, queries.dtype),
            pltpu.VMEM((KEY_VALUE_HEADS, 2, span, HEAD_SIZE), keys.dtype),
            pltpu.VMEM((rows, span), jnp.float32),
            pltpu.SMEM(doc_lengths.shape, doc_lengths.dtype),
            pltpu.SemaphoreType.DMA((2, KEY_VALUE_HEADS)),
            pltpu.SemaphoreType.DMA,
            pltpu.SemaphoreType.DMA,
            pltpu.SemaphoreType.DMA((most,)),
            pltpu.SemaphoreType.DMA((reach, KEY_VALUE_HEADS)),
        ],
        cost_estimate=pl.CostEstimate(
            flops=flops,
            bytes_accessed=2 * (queries.size * 2 + keys.size * 2),
            transcendentals=rows * span * QUERY_HEADS,
        ),
        compiler_params=pltpu.CompilerParams(
            collective_id=0, has_side_effects=True, vmem_limit_bytes=60 * 1024 * 1024
        ),
    )(queries, keys, values, doc_lengths)


def solution(mesh):
    in_specs = (
        P(("dp", "blk", "uly"), None),
        P(("dp", "blk", "uly"), None),
        P(("dp", "blk", "uly"), None),
        P("dp"),
    )
    out_specs = P(("dp", "blk", "uly"), None)
    uly = mesh.shape["uly"]
    blocks = mesh.shape["blk"] * uly
    return jax.shard_map(
        functools.partial(per_device, uly, blocks),
        mesh=mesh, in_specs=in_specs, out_specs=out_specs, check_vma=False,
    )
```

```python
import functools
import math

import jax
import jax.numpy as jnp
from jax import lax
from jax.experimental import pallas as pl
from jax.experimental.pallas import tpu as pltpu
from jax.sharding import PartitionSpec as P

QUERY_HEADS = 32
KEY_VALUE_HEADS = 8
HEAD_SIZE = 128
CYCLE = 2
GROUP = QUERY_HEADS // KEY_VALUE_HEADS

NEG_FILL = -1e30
AHEAD = 2

FOUR = (
    ((0, 4, None), (0, 1, None), (0, 2, None)),
    ((0, 4, None), (0, 1, None), (0, 2, None), (1, 2, None), (4, -1, 1)),
    ((0, 4, None), (0, 1, None), (1, 2, 0), (4, -2, None), (4, -1, 1), (3, -2, None)),
    ((0, 4, None), (1, 2, 0), (4, -1, None), (4, -2, None)),
)
FOUR_HOPS = (
    ((4,), (2, 3), (1,)),
    ((4, 1), (2, 3), ()),
    ((4, 1, 2), (3,), ()),
    ((4, 1, 2), (3,), ()),
)


def routes_for(uly, blocks):
    if CYCLE * uly == 4 and blocks % 4 == 0:
        return FOUR, FOUR_HOPS
    reach = CYCLE * uly
    direct = tuple((0, k, None) for k in range(1, reach + 1))
    return (direct,), ((tuple(range(1, reach + 1)),),)


def kernel(
    uly, blocks, q_hbm, k_hbm, v_hbm, len_hbm, o_ref,
    q_ref, kv_ref, bias_ref, len_ref,
    load_sem, q_sem, len_sem, send_sem, recv_sem,
):
    rows = q_ref.shape[0]
    reach = CYCLE * uly
    routes, hops = routes_for(uly, blocks)
    period = len(routes)
    b = lax.axis_index("blk") * uly + lax.axis_index("uly")
    role = lax.rem(b, period)

    def target(other):
        return {"blk": other // uly, "uly": lax.rem(other, uly)}

    def place(g, slot):
        return kv_ref.at[g, :, pl.ds((reach - slot) * rows, rows), :]

    def loads(g):
        cols = pl.ds(pl.multiple_of(g * HEAD_SIZE, HEAD_SIZE), HEAD_SIZE)
        here = pl.ds(reach * rows, rows)
        return [
            pltpu.make_async_copy(src.at[:, cols], kv_ref.at[g, i, here, :], load_sem.at[i, g])
            for i, src in enumerate((k_hbm, v_hbm))
        ]

    q_copy = pltpu.make_async_copy(q_hbm, q_ref, q_sem)
    len_copy = pltpu.make_async_copy(len_hbm, len_ref, len_sem)

    @pl.loop(0, KEY_VALUE_HEADS)
    def _(g):
        for copy in loads(g):
            copy.start()

    len_copy.start()
    q_copy.start()

    spans = sorted({abs(delta) for role_routes in routes for _, delta, _ in role_routes})
    barrier = pltpu.get_barrier_semaphore()
    expected = 0
    for span in spans:
        for other in (b + span, b - span):
            valid = (other >= 0) & (other < blocks)
            expected = expected + valid.astype(jnp.int32)

            @pl.when(valid)
            def _():
                pl.semaphore_signal(
                    barrier, inc=1, device_id=target(other), device_id_type=pl.DeviceIdType.MESH
                )

    for slot in range(1, reach + 1):

        @pl.when(b < slot)
        def _():
            @pl.loop(0, KEY_VALUE_HEADS)
            def _(g):
                kv_ref[g, :, pl.ds((reach - slot) * rows, rows), :] = jnp.zeros(
                    (2, rows, HEAD_SIZE), kv_ref.dtype
                )

    pl.semaphore_wait(barrier, expected)

    def start(r, g, from_slot):
        for n, (slot, delta, parity) in enumerate(routes[r]):
            if slot != from_slot:
                continue
            other = b + delta
            go = (other >= 0) & (other < blocks)
            if parity is not None:
                go = go & (lax.rem(g, 2) == parity)

            @pl.when(go)
            def _():
                pltpu.make_async_remote_copy(
                    src_ref=place(g, slot),
                    dst_ref=place(g, slot + delta),
                    send_sem=send_sem.at[n],
                    recv_sem=recv_sem.at[slot + delta - 1, g],
                    device_id=target(other),
                    device_id_type=pl.DeviceIdType.MESH,
                ).start()

    def receive(r, g, slots):
        for slot in slots:

            @pl.when(b >= slot)
            def _():
                pltpu.make_async_copy(
                    place(g, slot), place(g, slot), recv_sem.at[slot - 1, g]
                ).wait()
                start(r, g, slot)

    def all_sent(r):
        for n, (slot, delta, parity) in enumerate(routes[r]):
            other = b + delta
            heads = KEY_VALUE_HEADS if parity is None else KEY_VALUE_HEADS // 2

            @pl.when((b >= slot) & (other >= 0) & (other < blocks))
            def _():
                sent = kv_ref.at[pl.ds(0, heads), :, pl.ds((reach - slot) * rows, rows), :]
                pltpu.make_async_copy(sent, sent, send_sem.at[n]).wait()

    @pl.loop(0, KEY_VALUE_HEADS)
    def _(g):
        for copy in loads(g):
            copy.wait()

    for r in range(period):

        @pl.when(role == r)
        def _():
            @pl.loop(0, AHEAD)
            def _(g):
                start(r, g, 0)

    len_copy.wait()
    q_pos = b * rows + lax.broadcasted_iota(jnp.int32, (rows, 1), 0)
    first = jnp.zeros((rows, 1), jnp.int32)
    end = jnp.int32(0)
    for d in range(len_ref.shape[0]):
        end = end + len_ref[d]
        first = jnp.where(q_pos >= end, end, first)
    k_pos = (b - reach) * rows + lax.broadcasted_iota(jnp.int32, bias_ref.shape, 1)
    bias_ref[...] = jnp.where((k_pos <= q_pos) & (k_pos >= first), 0.0, NEG_FILL)

    q_copy.wait()
    factor = math.log2(math.e) / math.sqrt(HEAD_SIZE)

    def attend(g):
        keys = kv_ref[g, 0]
        values = kv_ref[g, 1]

        def cols(r):
            return pl.ds(pl.multiple_of((g * GROUP + r) * HEAD_SIZE, HEAD_SIZE), HEAD_SIZE)

        queries = jnp.concatenate([q_ref[:, cols(r)] for r in range(GROUP)], axis=0)
        scores = lax.dot_general(
            queries, keys, (((1,), (1,)), ((), ())), preferred_element_type=jnp.float32
        )
        parts = []
        for r in range(GROUP):
            part = scores[r * rows:(r + 1) * rows] + bias_ref[...]
            peak = jnp.max(part, axis=1, keepdims=True)
            parts.append(jnp.exp2((part - peak) * factor).astype(jnp.bfloat16))
        summed = jnp.dot(
            jnp.concatenate(parts, axis=0),
            jnp.concatenate([values, jnp.ones_like(values)], axis=1),
            preferred_element_type=jnp.float32,
        )
        result = (summed[:, :HEAD_SIZE] / summed[:, HEAD_SIZE:]).astype(o_ref.dtype)
        for r in range(GROUP):
            o_ref[:, cols(r)] = result[r * rows:(r + 1) * rows]

    depth = max(len(stages) for stages in hops)
    lag = sum(
        jnp.where(role == r, max(h for h, slots in enumerate(stages) if slots), 0)
        for r, stages in enumerate(hops)
    )

    @pl.loop(0, KEY_VALUE_HEADS + depth - 1)
    def _(t):
        for r, stages in enumerate(hops):

            @pl.when(role == r)
            def _():
                @pl.when(t + AHEAD < KEY_VALUE_HEADS)
                def _():
                    start(r, t + AHEAD, 0)

                for hop, slots in enumerate(stages):
                    if slots:

                        @pl.when((t >= hop) & (t - hop < KEY_VALUE_HEADS))
                        def _():
                            receive(r, t - hop, slots)

        @pl.when((t >= lag) & (t - lag < KEY_VALUE_HEADS))
        def _():
            attend(t - lag)

    for r in range(period):

        @pl.when(role == r)
        def _():
            all_sent(r)


def per_device(uly, blocks, queries, keys, values, doc_lengths):
    rows = queries.shape[0]
    reach = CYCLE * uly
    routes, _ = routes_for(uly, blocks)
    most = max(len(role_routes) for role_routes in routes)
    span = (reach + 1) * rows
    flops = 4 * rows * span * QUERY_HEADS * HEAD_SIZE
    return pl.pallas_call(
        functools.partial(kernel, uly, blocks),
        out_shape=pltpu.VMEM(queries.shape, queries.dtype),
        in_specs=[pl.BlockSpec(memory_space=pl.ANY)] * 4,
        out_specs=pl.BlockSpec(memory_space=pltpu.VMEM),
        scratch_shapes=[
            pltpu.VMEM(queries.shape, queries.dtype),
            pltpu.VMEM((KEY_VALUE_HEADS, 2, span, HEAD_SIZE), keys.dtype),
            pltpu.VMEM((rows, span), jnp.float32),
            pltpu.SMEM(doc_lengths.shape, doc_lengths.dtype),
            pltpu.SemaphoreType.DMA((2, KEY_VALUE_HEADS)),
            pltpu.SemaphoreType.DMA,
            pltpu.SemaphoreType.DMA,
            pltpu.SemaphoreType.DMA((most,)),
            pltpu.SemaphoreType.DMA((reach, KEY_VALUE_HEADS)),
        ],
        cost_estimate=pl.CostEstimate(
            flops=flops,
            bytes_accessed=2 * (queries.size * 2 + keys.size * 2),
            transcendentals=rows * span * QUERY_HEADS,
        ),
        compiler_params=pltpu.CompilerParams(
            collective_id=0, has_side_effects=True, vmem_limit_bytes=60 * 1024 * 1024
        ),
    )(queries, keys, values, doc_lengths)


def solution(mesh):
    in_specs = (
        P(("dp", "blk", "uly"), None),
        P(("dp", "blk", "uly"), None),
        P(("dp", "blk", "uly"), None),
        P("dp"),
    )
    out_specs = P(("dp", "blk", "uly"), None)
    uly = mesh.shape["uly"]
    blocks = mesh.shape["blk"] * uly
    return jax.shard_map(
        functools.partial(per_device, uly, blocks),
        mesh=mesh, in_specs=in_specs, out_specs=out_specs, check_vma=False,
    )
```

```python
import functools
import math

import jax
import jax.numpy as jnp
from jax import lax
from jax.experimental import pallas as pl
from jax.experimental.pallas import tpu as pltpu
from jax.sharding import PartitionSpec as P

QUERY_HEADS = 32
KEY_VALUE_HEADS = 8
HEAD_SIZE = 128
CYCLE = 2
GROUP = QUERY_HEADS // KEY_VALUE_HEADS

NEG_FILL = -1e30
AHEAD = 2

FOUR = (
    ((0, 1, None), (0, 4, None), (0, 2, None)),
    ((0, 1, None), (0, 4, None), (0, 2, None), (1, 2, None), (4, -1, 1)),
    ((0, 1, None), (0, 4, None), (1, 2, 0), (4, -2, None), (4, -1, 1), (3, -2, None)),
    ((0, 4, None), (1, 2, 0), (4, -1, None), (4, -2, None)),
)
FOUR_HOPS = (
    ((4,), (2, 3), (1,)),
    ((4, 1), (2, 3), ()),
    ((4, 1, 2), (3,), ()),
    ((4, 1, 2), (3,), ()),
)


def routes_for(uly, blocks):
    if CYCLE * uly == 4 and blocks % 4 == 0:
        return FOUR, FOUR_HOPS
    reach = CYCLE * uly
    direct = tuple((0, k, None) for k in range(1, reach + 1))
    return (direct,), ((tuple(range(1, reach + 1)),),)


def kernel(
    uly, blocks, q_hbm, k_hbm, v_hbm, len_hbm, o_ref,
    q_ref, kv_ref, bias_ref, len_ref,
    load_sem, q_sem, len_sem, send_sem, recv_sem,
):
    rows = q_ref.shape[0]
    reach = CYCLE * uly
    routes, hops = routes_for(uly, blocks)
    period = len(routes)
    b = lax.axis_index("blk") * uly + lax.axis_index("uly")
    role = lax.rem(b, period)

    def target(other):
        return {"blk": other // uly, "uly": lax.rem(other, uly)}

    def place(g, slot):
        return kv_ref.at[g, :, pl.ds((reach - slot) * rows, rows), :]

    def loads(g):
        cols = pl.ds(pl.multiple_of(g * HEAD_SIZE, HEAD_SIZE), HEAD_SIZE)
        here = pl.ds(reach * rows, rows)
        return [
            pltpu.make_async_copy(src.at[:, cols], kv_ref.at[g, i, here, :], load_sem.at[i, g])
            for i, src in enumerate((k_hbm, v_hbm))
        ]

    q_copy = pltpu.make_async_copy(q_hbm, q_ref, q_sem)
    len_copy = pltpu.make_async_copy(len_hbm, len_ref, len_sem)

    @pl.loop(0, KEY_VALUE_HEADS)
    def _(g):
        for copy in loads(g):
            copy.start()

    len_copy.start()
    q_copy.start()

    spans = sorted({abs(delta) for role_routes in routes for _, delta, _ in role_routes})
    barrier = pltpu.get_barrier_semaphore()
    expected = 0
    for span in spans:
        for other in (b + span, b - span):
            valid = (other >= 0) & (other < blocks)
            expected = expected + valid.astype(jnp.int32)

            @pl.when(valid)
            def _():
                pl.semaphore_signal(
                    barrier, inc=1, device_id=target(other), device_id_type=pl.DeviceIdType.MESH
                )

    for slot in range(1, reach + 1):

        @pl.when(b < slot)
        def _():
            @pl.loop(0, KEY_VALUE_HEADS)
            def _(g):
                kv_ref[g, :, pl.ds((reach - slot) * rows, rows), :] = jnp.zeros(
                    (2, rows, HEAD_SIZE), kv_ref.dtype
                )

    pl.semaphore_wait(barrier, expected)

    def start(r, g, from_slot):
        for n, (slot, delta, parity) in enumerate(routes[r]):
            if slot != from_slot:
                continue
            other = b + delta
            go = (other >= 0) & (other < blocks)
            if parity is not None:
                go = go & (lax.rem(g, 2) == parity)

            @pl.when(go)
            def _():
                pltpu.make_async_remote_copy(
                    src_ref=place(g, slot),
                    dst_ref=place(g, slot + delta),
                    send_sem=send_sem.at[n],
                    recv_sem=recv_sem.at[slot + delta - 1, g],
                    device_id=target(other),
                    device_id_type=pl.DeviceIdType.MESH,
                ).start()

    def receive(r, g, slots):
        for slot in slots:

            @pl.when(b >= slot)
            def _():
                pltpu.make_async_copy(
                    place(g, slot), place(g, slot), recv_sem.at[slot - 1, g]
                ).wait()
                start(r, g, slot)

    def all_sent(r):
        for n, (slot, delta, parity) in enumerate(routes[r]):
            other = b + delta
            heads = KEY_VALUE_HEADS if parity is None else KEY_VALUE_HEADS // 2

            @pl.when((b >= slot) & (other >= 0) & (other < blocks))
            def _():
                sent = kv_ref.at[pl.ds(0, heads), :, pl.ds((reach - slot) * rows, rows), :]
                pltpu.make_async_copy(sent, sent, send_sem.at[n]).wait()

    @pl.loop(0, KEY_VALUE_HEADS)
    def _(g):
        for copy in loads(g):
            copy.wait()

    for r in range(period):

        @pl.when(role == r)
        def _():
            @pl.loop(0, AHEAD)
            def _(g):
                start(r, g, 0)

    len_copy.wait()
    q_pos = b * rows + lax.broadcasted_iota(jnp.int32, (rows, 1), 0)
    first = jnp.zeros((rows, 1), jnp.int32)
    end = jnp.int32(0)
    for d in range(len_ref.shape[0]):
        end = end + len_ref[d]
        first = jnp.where(q_pos >= end, end, first)
    k_pos = (b - reach) * rows + lax.broadcasted_iota(jnp.int32, bias_ref.shape, 1)
    bias_ref[...] = jnp.where((k_pos <= q_pos) & (k_pos >= first), 0.0, NEG_FILL)

    q_copy.wait()
    factor = math.log2(math.e) / math.sqrt(HEAD_SIZE)

    def attend(g):
        keys = kv_ref[g, 0]
        values = kv_ref[g, 1]

        def cols(r):
            return pl.ds(pl.multiple_of((g * GROUP + r) * HEAD_SIZE, HEAD_SIZE), HEAD_SIZE)

        queries = jnp.concatenate([q_ref[:, cols(r)] for r in range(GROUP)], axis=0)
        scores = lax.dot_general(
            queries, keys, (((1,), (1,)), ((), ())), preferred_element_type=jnp.float32
        )
        parts = []
        for r in range(GROUP):
            part = scores[r * rows:(r + 1) * rows] + bias_ref[...]
            peak = jnp.max(part, axis=1, keepdims=True)
            parts.append(jnp.exp2((part - peak) * factor).astype(jnp.bfloat16))
        summed = jnp.dot(
            jnp.concatenate(parts, axis=0),
            jnp.concatenate([values, jnp.ones_like(values)], axis=1),
            preferred_element_type=jnp.float32,
        )
        result = (summed[:, :HEAD_SIZE] / summed[:, HEAD_SIZE:]).astype(o_ref.dtype)
        for r in range(GROUP):
            o_ref[:, cols(r)] = result[r * rows:(r + 1) * rows]

    depth = max(len(stages) for stages in hops)
    lag = sum(
        jnp.where(role == r, max(h for h, slots in enumerate(stages) if slots), 0)
        for r, stages in enumerate(hops)
    )

    @pl.loop(0, KEY_VALUE_HEADS + depth - 1)
    def _(t):
        for r, stages in enumerate(hops):

            @pl.when(role == r)
            def _():
                @pl.when(t + AHEAD < KEY_VALUE_HEADS)
                def _():
                    start(r, t + AHEAD, 0)

                for hop, slots in enumerate(stages):
                    if slots:

                        @pl.when((t >= hop) & (t - hop < KEY_VALUE_HEADS))
                        def _():
                            receive(r, t - hop, slots)

        @pl.when((t >= lag) & (t - lag < KEY_VALUE_HEADS))
        def _():
            attend(t - lag)

    for r in range(period):

        @pl.when(role == r)
        def _():
            all_sent(r)


def per_device(uly, blocks, queries, keys, values, doc_lengths):
    rows = queries.shape[0]
    reach = CYCLE * uly
    routes, _ = routes_for(uly, blocks)
    most = max(len(role_routes) for role_routes in routes)
    span = (reach + 1) * rows
    flops = 4 * rows * span * QUERY_HEADS * HEAD_SIZE
    return pl.pallas_call(
        functools.partial(kernel, uly, blocks),
        out_shape=pltpu.VMEM(queries.shape, queries.dtype),
        in_specs=[pl.BlockSpec(memory_space=pl.ANY)] * 4,
        out_specs=pl.BlockSpec(memory_space=pltpu.VMEM),
        scratch_shapes=[
            pltpu.VMEM(queries.shape, queries.dtype),
            pltpu.VMEM((KEY_VALUE_HEADS, 2, span, HEAD_SIZE), keys.dtype),
            pltpu.VMEM((rows, span), jnp.float32),
            pltpu.SMEM(doc_lengths.shape, doc_lengths.dtype),
            pltpu.SemaphoreType.DMA((2, KEY_VALUE_HEADS)),
            pltpu.SemaphoreType.DMA,
            pltpu.SemaphoreType.DMA,
            pltpu.SemaphoreType.DMA((most,)),
            pltpu.SemaphoreType.DMA((reach, KEY_VALUE_HEADS)),
        ],
        cost_estimate=pl.CostEstimate(
            flops=flops,
            bytes_accessed=2 * (queries.size * 2 + keys.size * 2),
            transcendentals=rows * span * QUERY_HEADS,
        ),
        compiler_params=pltpu.CompilerParams(
            collective_id=0, has_side_effects=True, vmem_limit_bytes=60 * 1024 * 1024
        ),
    )(queries, keys, values, doc_lengths)


def solution(mesh):
    in_specs = (
        P(("dp", "blk", "uly"), None),
        P(("dp", "blk", "uly"), None),
        P(("dp", "blk", "uly"), None),
        P("dp"),
    )
    out_specs = P(("dp", "blk", "uly"), None)
    uly = mesh.shape["uly"]
    blocks = mesh.shape["blk"] * uly
    return jax.shard_map(
        functools.partial(per_device, uly, blocks),
        mesh=mesh, in_specs=in_specs, out_specs=out_specs, check_vma=False,
    )
```

```python
import functools
import math

import jax
import jax.numpy as jnp
from jax import lax
from jax.experimental import pallas as pl
from jax.experimental.pallas import tpu as pltpu
from jax.sharding import PartitionSpec as P

QUERY_HEADS = 32
KEY_VALUE_HEADS = 8
HEAD_SIZE = 128
CYCLE = 2
GROUP = QUERY_HEADS // KEY_VALUE_HEADS

NEG_FILL = -1e30
AHEAD = 2

FOUR = (
    ((0, 1, None), (0, 4, None), (0, 2, None)),
    ((0, 1, None), (0, 4, None), (0, 2, None), (1, 2, None), (4, -1, 1)),
    ((0, 1, None), (0, 4, None), (1, 2, 0), (4, -2, None), (4, -1, 1), (3, -2, None)),
    ((0, 4, None), (1, 2, 0), (4, -1, None), (4, -2, None)),
)
FOUR_HOPS = (
    ((), (), (4, 2, 3, 1)),
    ((4, 1), (2, 3), ()),
    ((4, 1, 2), (3,), ()),
    ((4, 1, 2), (3,), ()),
)


def routes_for(uly, blocks):
    if CYCLE * uly == 4 and blocks % 4 == 0:
        return FOUR, FOUR_HOPS
    reach = CYCLE * uly
    direct = tuple((0, k, None) for k in range(1, reach + 1))
    return (direct,), ((tuple(range(1, reach + 1)),),)


def kernel(
    uly, blocks, q_hbm, k_hbm, v_hbm, len_hbm, o_ref,
    q_ref, kv_ref, bias_ref, len_ref,
    load_sem, q_sem, len_sem, send_sem, recv_sem,
):
    rows = q_ref.shape[0]
    reach = CYCLE * uly
    routes, hops = routes_for(uly, blocks)
    period = len(routes)
    b = lax.axis_index("blk") * uly + lax.axis_index("uly")
    role = lax.rem(b, period)

    def target(other):
        return {"blk": other // uly, "uly": lax.rem(other, uly)}

    def place(g, slot):
        return kv_ref.at[g, :, pl.ds((reach - slot) * rows, rows), :]

    def loads(g):
        cols = pl.ds(pl.multiple_of(g * HEAD_SIZE, HEAD_SIZE), HEAD_SIZE)
        here = pl.ds(reach * rows, rows)
        return [
            pltpu.make_async_copy(src.at[:, cols], kv_ref.at[g, i, here, :], load_sem.at[i, g])
            for i, src in enumerate((k_hbm, v_hbm))
        ]

    q_copy = pltpu.make_async_copy(q_hbm, q_ref, q_sem)
    len_copy = pltpu.make_async_copy(len_hbm, len_ref, len_sem)

    @pl.loop(0, KEY_VALUE_HEADS)
    def _(g):
        for copy in loads(g):
            copy.start()

    len_copy.start()
    q_copy.start()

    spans = sorted({abs(delta) for role_routes in routes for _, delta, _ in role_routes})
    barrier = pltpu.get_barrier_semaphore()
    expected = 0
    for span in spans:
        for other in (b + span, b - span):
            valid = (other >= 0) & (other < blocks)
            expected = expected + valid.astype(jnp.int32)

            @pl.when(valid)
            def _():
                pl.semaphore_signal(
                    barrier, inc=1, device_id=target(other), device_id_type=pl.DeviceIdType.MESH
                )

    for slot in range(1, reach + 1):

        @pl.when(b < slot)
        def _():
            @pl.loop(0, KEY_VALUE_HEADS)
            def _(g):
                kv_ref[g, :, pl.ds((reach - slot) * rows, rows), :] = jnp.zeros(
                    (2, rows, HEAD_SIZE), kv_ref.dtype
                )

    pl.semaphore_wait(barrier, expected)

    def start(r, g, from_slot):
        for n, (slot, delta, parity) in enumerate(routes[r]):
            if slot != from_slot:
                continue
            other = b + delta
            go = (other >= 0) & (other < blocks)
            if parity is not None:
                go = go & (lax.rem(g, 2) == parity)

            @pl.when(go)
            def _():
                pltpu.make_async_remote_copy(
                    src_ref=place(g, slot),
                    dst_ref=place(g, slot + delta),
                    send_sem=send_sem.at[n],
                    recv_sem=recv_sem.at[slot + delta - 1, g],
                    device_id=target(other),
                    device_id_type=pl.DeviceIdType.MESH,
                ).start()

    def receive(r, g, slots):
        for slot in slots:

            @pl.when(b >= slot)
            def _():
                pltpu.make_async_copy(
                    place(g, slot), place(g, slot), recv_sem.at[slot - 1, g]
                ).wait()
                start(r, g, slot)

    def all_sent(r):
        for n, (slot, delta, parity) in enumerate(routes[r]):
            other = b + delta
            heads = KEY_VALUE_HEADS if parity is None else KEY_VALUE_HEADS // 2

            @pl.when((b >= slot) & (other >= 0) & (other < blocks))
            def _():
                sent = kv_ref.at[pl.ds(0, heads), :, pl.ds((reach - slot) * rows, rows), :]
                pltpu.make_async_copy(sent, sent, send_sem.at[n]).wait()

    @pl.loop(0, KEY_VALUE_HEADS)
    def _(g):
        for copy in loads(g):
            copy.wait()

    for r in range(period):

        @pl.when(role == r)
        def _():
            @pl.loop(0, AHEAD)
            def _(g):
                start(r, g, 0)

    len_copy.wait()
    q_pos = b * rows + lax.broadcasted_iota(jnp.int32, (rows, 1), 0)
    first = jnp.zeros((rows, 1), jnp.int32)
    end = jnp.int32(0)
    for d in range(len_ref.shape[0]):
        end = end + len_ref[d]
        first = jnp.where(q_pos >= end, end, first)
    k_pos = (b - reach) * rows + lax.broadcasted_iota(jnp.int32, bias_ref.shape, 1)
    bias_ref[...] = jnp.where((k_pos <= q_pos) & (k_pos >= first), 0.0, NEG_FILL)

    q_copy.wait()
    factor = math.log2(math.e) / math.sqrt(HEAD_SIZE)

    def attend(g):
        keys = kv_ref[g, 0]
        values = kv_ref[g, 1]

        def cols(r):
            return pl.ds(pl.multiple_of((g * GROUP + r) * HEAD_SIZE, HEAD_SIZE), HEAD_SIZE)

        queries = jnp.concatenate([q_ref[:, cols(r)] for r in range(GROUP)], axis=0)
        scores = lax.dot_general(
            queries, keys, (((1,), (1,)), ((), ())), preferred_element_type=jnp.float32
        )
        parts = []
        for r in range(GROUP):
            part = scores[r * rows:(r + 1) * rows] + bias_ref[...]
            peak = jnp.max(part, axis=1, keepdims=True)
            parts.append(jnp.exp2((part - peak) * factor).astype(jnp.bfloat16))
        summed = jnp.dot(
            jnp.concatenate(parts, axis=0),
            jnp.concatenate([values, jnp.ones_like(values)], axis=1),
            preferred_element_type=jnp.float32,
        )
        result = (summed[:, :HEAD_SIZE] / summed[:, HEAD_SIZE:]).astype(o_ref.dtype)
        for r in range(GROUP):
            o_ref[:, cols(r)] = result[r * rows:(r + 1) * rows]

    depth = max(len(stages) for stages in hops)
    lag = sum(
        jnp.where(role == r, max(h for h, slots in enumerate(stages) if slots), 0)
        for r, stages in enumerate(hops)
    )

    @pl.loop(0, KEY_VALUE_HEADS + depth - 1)
    def _(t):
        for r, stages in enumerate(hops):

            @pl.when(role == r)
            def _():
                @pl.when(t + AHEAD < KEY_VALUE_HEADS)
                def _():
                    start(r, t + AHEAD, 0)

                for hop, slots in enumerate(stages):
                    if slots:

                        @pl.when((t >= hop) & (t - hop < KEY_VALUE_HEADS))
                        def _():
                            receive(r, t - hop, slots)

        @pl.when((t >= lag) & (t - lag < KEY_VALUE_HEADS))
        def _():
            attend(t - lag)

    for r in range(period):

        @pl.when(role == r)
        def _():
            all_sent(r)


def per_device(uly, blocks, queries, keys, values, doc_lengths):
    rows = queries.shape[0]
    reach = CYCLE * uly
    routes, _ = routes_for(uly, blocks)
    most = max(len(role_routes) for role_routes in routes)
    span = (reach + 1) * rows
    flops = 4 * rows * span * QUERY_HEADS * HEAD_SIZE
    return pl.pallas_call(
        functools.partial(kernel, uly, blocks),
        out_shape=pltpu.VMEM(queries.shape, queries.dtype),
        in_specs=[pl.BlockSpec(memory_space=pl.ANY)] * 4,
        out_specs=pl.BlockSpec(memory_space=pltpu.VMEM),
        scratch_shapes=[
            pltpu.VMEM(queries.shape, queries.dtype),
            pltpu.VMEM((KEY_VALUE_HEADS, 2, span, HEAD_SIZE), keys.dtype),
            pltpu.VMEM((rows, span), jnp.float32),
            pltpu.SMEM(doc_lengths.shape, doc_lengths.dtype),
            pltpu.SemaphoreType.DMA((2, KEY_VALUE_HEADS)),
            pltpu.SemaphoreType.DMA,
            pltpu.SemaphoreType.DMA,
            pltpu.SemaphoreType.DMA((most,)),
            pltpu.SemaphoreType.DMA((reach, KEY_VALUE_HEADS)),
        ],
        cost_estimate=pl.CostEstimate(
            flops=flops,
            bytes_accessed=2 * (queries.size * 2 + keys.size * 2),
            transcendentals=rows * span * QUERY_HEADS,
        ),
        compiler_params=pltpu.CompilerParams(
            collective_id=0, has_side_effects=True, vmem_limit_bytes=60 * 1024 * 1024
        ),
    )(queries, keys, values, doc_lengths)


def solution(mesh):
    in_specs = (
        P(("dp", "blk", "uly"), None),
        P(("dp", "blk", "uly"), None),
        P(("dp", "blk", "uly"), None),
        P("dp"),
    )
    out_specs = P(("dp", "blk", "uly"), None)
    uly = mesh.shape["uly"]
    blocks = mesh.shape["blk"] * uly
    return jax.shard_map(
        functools.partial(per_device, uly, blocks),
        mesh=mesh, in_specs=in_specs, out_specs=out_specs, check_vma=False,
    )
```
